32 devices in a mesh: gz: 2 (over x), pr: 4 (over y, core), pc: 4 (over z).
Axes of the slice: x: 2, y: 2, z: 4, core: 2. Of those that a mesh axis runs over, the one named last changes fastest.
Arguments:
- sep_rhs: bfloat16 [4, 3, 128, 128], P('pr'), may hold values from -6 to 6
- diag_inverse: bfloat16 [4, 3, 128, 128], P('pr'), may hold values from -0.5 to 0.5
- off_blocks: bfloat16 [4, 3, 3, 4, 128, 128], P('pr', None, None, 'pc'), may hold values from -0.21875 to 0.21875
- pattern: int32 [12, 12], replicated, may hold values 0 or 1
- sub_solution: bfloat16 [2, 4, 4, 1024, 128], P('gz', 'pr', 'pc'), may hold values from -6 to 6
- couple_low: bfloat16 [2, 4, 4, 384, 1024], P('gz', 'pr', 'pc'), may hold values from -0.0625 to 0.0625
- couple_up: bfloat16 [2, 4, 4, 1024, 384], P('gz', 'pr', 'pc'), may hold values from -0.3125 to 0.3125
Outputs:
- sep_solution: bfloat16 [4, 3, 128, 128], P('pr')
- sub_result: bfloat16 [2, 4, 4, 1024, 128], P('gz', 'pr', 'pc')
The draws below stay inside these ranges and needn't reach their ends.
Inputs may be any that keep to these rules, and one draw needn't show every extreme that they name: `pattern`: only entries [i, j] with i // 4 > j // 4 are read; 1 marks a nonzero block.
All inputs are finite; a program needn't handle non-finite values.
Results may differ from the reference program's by a relative error of at most 0.02.
Values may be sent and summed in bfloat16 or wider, within the bound.
No kernel may reach another device: no remote copies, remote signals or barrier semaphores. Data moves between devices by JAX's collectives and lax.ppermute only.
A program may use at most 64 MiB of HBM per device.

```python
import jax
import jax.numpy as jnp
from jax import lax

S = 128
R = 128
SUB = 1024
RB = 3
NS = 12
CB = 3
N_GZ = 2
N_PR = 4
N_PC = 4


def with_ends(values, rng, least, largest):
    longest = values.shape.index(max(values.shape))
    spots = []
    for shift in (0, 1):
        where = [jax.random.randint(jax.random.fold_in(rng, axis), (), 0, length) for axis, length in enumerate(values.shape)]
        where[longest] = (where[longest] + shift) % values.shape[longest]
        spots.append(tuple(where))
    return values.at[spots[0]].set(least).at[spots[1]].set(largest)


def block_scale(key, shape, split, least, top_value):
    factor_of, own = 1.0, jax.random.fold_in(key, 6)
    for dim, shards_of in split:
        draws = jnp.exp(jax.random.uniform(jax.random.fold_in(own, dim), (shards_of,), jnp.float32, least / len(split), top_value / len(split)))
        factor_of = factor_of * jnp.repeat(draws, shape[dim] // shards_of).reshape([-1 if axis == dim else 1 for axis in range(len(shape))])
    return factor_of


def bell_draw(rng, shape, scale, bound, pieces=(), held_as=jnp.bfloat16):
    loudness = block_scale(rng, shape, pieces, -0.22, 0.18) if pieces else 1.0
    entries = jax.random.normal(rng, shape, jnp.float32) * scale * loudness
    return jnp.minimum(jnp.maximum(entries, -bound), bound).astype(held_as)


def setup_inputs(seed: int = 0) -> dict:
    streams_of = jax.random.split(jax.random.key(seed), 8)
    sep_rhs = bell_draw(streams_of[0], (N_PR, RB, S, R), 1.0, 6.0, ((0, 4),))
    diag_inverse = bell_draw(streams_of[1], (N_PR, RB, S, S), S ** -0.5, 0.5, ((0, 4),))
    off_blocks = bell_draw(streams_of[2], (N_PR, RB, CB, N_PC, S, S), (S * NS // 2) ** -0.5, 0.21875, ((0, 4), (3, 4)))
    pattern = with_ends((jax.random.randint(streams_of[3], (NS, NS), 0, 2) < 1).astype(jnp.int32), jax.random.fold_in(streams_of[3], 1), 0, 1)
    sub_solution = bell_draw(streams_of[4], (N_GZ, N_PR, N_PC, SUB, R), 1.0, 6.0, ((0, 2), (1, 4), (2, 4)))
    couple_low = bell_draw(streams_of[5], (N_GZ, N_PR, N_PC, RB * S, SUB), (SUB * N_GZ * N_PC) ** -0.5, 0.0625, ((0, 2), (1, 4), (2, 4)))
    couple_up = bell_draw(streams_of[6], (N_GZ, N_PR, N_PC, SUB, RB * S), (RB * S) ** -0.5, 0.3125, ((0, 2), (1, 4), (2, 4)))
    return {"sep_rhs": sep_rhs, "diag_inverse": diag_inverse, "off_blocks": off_blocks, "pattern": pattern, "sub_solution": sub_solution, "couple_low": couple_low, "couple_up": couple_up}


def couple_term(pair_args):
    return jnp.dot(pair_args[0], pair_args[1], preferred_element_type=jnp.float32)


def reference(sep_rhs, diag_inverse, off_blocks, pattern, sub_solution, couple_low, couple_up):
    count_all = N_GZ * N_PR * N_PC
    low_flat = couple_low.reshape(count_all, RB * S, SUB)
    sub_flat = sub_solution.reshape(count_all, SUB, R)
    terms = lax.map(couple_term, (low_flat, sub_flat))
    terms = terms.reshape(N_GZ, N_PR, N_PC, RB, S, R)
    summed = jnp.sum(jnp.sum(terms, axis=2), axis=0)
    fed_rhs = sep_rhs.astype(jnp.float32) - summed
    y_list = []
    for i in range(NS):
        prow, arow = i % N_PR, i // N_PR
        parts = [jnp.zeros((S, R), jnp.float32) for q in range(N_PC)]
        for j in range(NS):
            if j // N_PR < arow:
                product = jnp.dot(off_blocks[prow, arow, j // N_PC, j % N_PC], y_list[j], preferred_element_type=jnp.float32)
                parts[j % N_PC] = parts[j % N_PC] + jnp.where(pattern[i, j] == 1, product, 0.0)
        lowsum = jnp.zeros((S, R), jnp.float32)
        for q in range(N_PC):
            lowsum = lowsum + parts[q].astype(jnp.bfloat16).astype(jnp.float32)
        resid = (fed_rhs[prow, arow] - lowsum).astype(jnp.bfloat16)
        y_list.append(jnp.dot(diag_inverse[prow, arow], resid, preferred_element_type=jnp.float32).astype(jnp.bfloat16))
    x_list = [None] * NS
    for i in range(NS - 1, -1, -1):
        prow, arow = i % N_PR, i // N_PR
        parts = [jnp.zeros((S, R), jnp.float32) for q in range(N_PC)]
        for j in range(NS):
            if j // N_PR > arow:
                product = jnp.dot(off_blocks[prow, arow, j // N_PC, j % N_PC], x_list[j], preferred_element_type=jnp.float32)
                parts[j % N_PC] = parts[j % N_PC] + jnp.where(pattern[j, i] == 1, product, 0.0)
        upsum = jnp.zeros((S, R), jnp.float32)
        for q in range(N_PC):
            upsum = upsum + parts[q].astype(jnp.bfloat16).astype(jnp.float32)
        x_list[i] = (y_list[i].astype(jnp.float32) - upsum).astype(jnp.bfloat16)
    stacked = jnp.stack(x_list).reshape(RB, N_PR, S, R)
    sep_solution = jnp.transpose(stacked, (1, 0, 2, 3))
    x_rows = sep_solution.reshape(N_PR, RB * S, R)
    up_flat = couple_up.reshape(count_all, SUB, RB * S)
    owners = (jnp.arange(count_all, dtype=jnp.int32) // N_PC) % N_PR

    def remove_term(pair_args):
        own_rows = lax.dynamic_index_in_dim(x_rows, pair_args[2], 0, keepdims=False)
        product = jnp.dot(pair_args[0], own_rows, preferred_element_type=jnp.float32)
        return (pair_args[1].astype(jnp.float32) - product).astype(jnp.bfloat16)

    sub_result = lax.map(remove_term, (up_flat, sub_flat, owners))
    return sep_solution, sub_result.reshape(N_GZ, N_PR, N_PC, SUB, R)
```

```python
import jax
import jax.numpy as jnp
from jax import lax
from jax.experimental import pallas as pl
from jax.experimental.pallas import tpu as pltpu
from jax.sharding import PartitionSpec as P

FIRST, MIDDLE, LAST = range(3)
VMEM = pl.BlockSpec(memory_space=pltpu.VMEM)
SMEM = pl.BlockSpec(memory_space=pltpu.SMEM)


def dot(a, b):
    return jnp.dot(a, b, preferred_element_type=jnp.float32)


def hop(x, axis, offset):
    size = lax.axis_size(axis)
    return lax.ppermute(x, axis, [(i, i ^ offset) for i in range(size)])


def spread(x, axis):
    held = {0: x}
    bit = lax.axis_size(axis) // 2
    while bit:
        held.update({k ^ bit: hop(value, axis, bit) for k, value in list(held.items())})
        bit //= 2
    return [held[k] for k in range(len(held))]


def spread_direct(x, axis):
    return [x] + [hop(x, axis, k) for k in range(1, lax.axis_size(axis))]


def call(kernel, outs, args, scratch=(), in_specs=None):
    return pl.pallas_call(
        kernel,
        out_shape=outs,
        in_specs=in_specs or [VMEM] * len(args),
        out_specs=[VMEM] * len(outs),
        scratch_shapes=list(scratch),
        compiler_params=pltpu.CompilerParams(vmem_limit_bytes=48 * 1024 * 1024),
    )(*args)


def per_device(sep_rhs, diag_inverse, off_blocks, pattern, sub_solution, couple_low, couple_up):
    rows, cols = lax.axis_size("pr"), lax.axis_size("pc")
    rhs, inverse, blocks = sep_rhs[0], diag_inverse[0], off_blocks[0, :, :, 0]
    sub, low, up = sub_solution[0, 0, 0], couple_low[0, 0, 0], couple_up[0, 0, 0]
    levels, width, count = rhs.shape
    per = blocks.shape[1] // levels
    assert levels == 3 and per * cols == rows
    bf16, f32 = jnp.bfloat16, jnp.float32

    def shaped(*shape):
        return jax.ShapeDtypeStruct(shape, bf16)

    def start_kernel(pattern_ref, low_ref, sub_ref, blocks_ref, part_ref, mid_a_ref, mid_b_ref, last_ref, first_ref):
        row, col = lax.axis_index("pr"), lax.axis_index("pc")

        def masked(level, b):
            i, j = level * rows + row, b * cols + col
            mark = pattern_ref[i, j] if b // per < level else pattern_ref[j, i]
            return jnp.where(mark == 1, blocks_ref[level, b], jnp.zeros((width, width), bf16))

        part_ref[...] = dot(low_ref[...], sub_ref[...]).astype(bf16).reshape(levels, width, count)
        for m in range(per):
            mid_a_ref[m] = masked(MIDDLE, m)
            mid_b_ref[m] = masked(MIDDLE, LAST * per + m)
        for m in range(2 * per):
            last_ref[m] = masked(LAST, m)
            first_ref[m] = masked(FIRST, per + m)

    part, mid_a, mid_b, last, first = call(
        start_kernel,
        [shaped(levels, width, count), shaped(per, width, width), shaped(per, width, width),
         shaped(2 * per, width, width), shaped(2 * per, width, width)],
        [pattern, low, sub, blocks],
        in_specs=[SMEM, VMEM, VMEM, VMEM],
    )

    bit = 1
    while bit < lax.axis_size("gz"):
        part = part + hop(part, "gz", bit)
        bit *= 2
    parts = spread_direct(part, "pc")
    mid_a = jnp.concatenate(spread_direct(mid_a, "pc") + [inverse[MIDDLE][None]])
    mid_a = spread(mid_a, "pr")
    mid_b = spread(jnp.concatenate(spread_direct(mid_b, "pc")), "pr")
    last = spread_direct(last, "pc")
    first = spread_direct(first, "pc")

    def solve_first(rhs_ref, inverse_ref, *refs):
        out_ref, resid_ref = refs[cols:]
        for level in range(levels):
            total = sum(ref[level].astype(f32) for ref in refs[:cols])
            resid = (rhs_ref[level].astype(f32) - total).astype(bf16)
            if level == FIRST:
                out_ref[0] = dot(inverse_ref[...], resid).astype(bf16)
            elif level == MIDDLE:
                out_ref[1] = resid
            else:
                resid_ref[...] = resid

    solved, resid_last = call(
        solve_first, [shaped(2, width, count), shaped(width, count)], [rhs, inverse[FIRST], *parts]
    )
    gathered = spread(solved, "pr")

    def columns(refs_by_col, indices):
        return jnp.concatenate([ref[m] for ref in refs_by_col for m in indices], axis=1)

    def solve_forward(inverse_ref, resid_ref, *refs):
        solved_refs, mid_refs, last_refs = refs[:rows], refs[rows:2 * rows], refs[2 * rows:2 * rows + cols]
        x_last_ref, y_mid_ref, y_first_ref = refs[2 * rows + cols:]
        row, col = lax.axis_index("pr"), lax.axis_index("pc")
        for k in range(rows):
            y_first_ref[row ^ k] = solved_refs[k][0]
        y_first = [y_first_ref[m * cols + (col ^ k)] for k in range(cols) for m in range(per)]
        stacked = jnp.concatenate(y_first, axis=0)
        for k in range(rows):
            factor = jnp.concatenate([mid_refs[k][j] for j in range(cols * per)], axis=1)
            resid = (solved_refs[k][1].astype(f32) - dot(factor, stacked)).astype(bf16)
            y_mid_ref[row ^ k] = dot(mid_refs[k][cols * per], resid).astype(bf16)
        total = dot(columns(last_refs, range(per)), stacked)
        y_mid = [y_mid_ref[m * cols + (col ^ k)] for k in range(cols) for m in range(per)]
        total += dot(columns(last_refs, range(per, 2 * per)), jnp.concatenate(y_mid, axis=0))
        resid = (resid_ref[...].astype(f32) - total).astype(bf16)
        x_last_ref[...] = dot(inverse_ref[...], resid).astype(bf16)

    x_last, y_mid = call(
        solve_forward,
        [shaped(width, count), shaped(rows, width, count)],
        [inverse[LAST], resid_last, *gathered, *mid_a, *last],
        scratch=[pltpu.VMEM((rows, width, count), bf16)],
    )
    x_lasts = spread(x_last, "pr")

    def solve_backward(solved_ref, y_mid_ref, up_ref, sub_ref, *refs):
        x_last_refs, mid_refs, first_refs = refs[:rows], refs[rows:2 * rows], refs[2 * rows:2 * rows + cols]
        solution_ref, result_ref, x_last_all, x_mid_all = refs[2 * rows + cols:]
        row, col = lax.axis_index("pr"), lax.axis_index("pc")
        for k in range(rows):
            x_last_all[row ^ k] = x_last_refs[k][...]
        stacked = jnp.concatenate([x_last_all[m * cols + (col ^ k)] for k in range(cols) for m in range(per)], axis=0)
        for k in range(rows):
            factor = jnp.concatenate([mid_refs[k][j] for j in range(cols * per)], axis=1)
            x_mid_all[row ^ k] = (y_mid_ref[row ^ k].astype(f32) - dot(factor, stacked)).astype(bf16)
        x_mid = [x_mid_all[m * cols + (col ^ k)] for k in range(cols) for m in range(per)]
        total = dot(columns(first_refs, range(per, 2 * per)), stacked)
        total += dot(columns(first_refs, range(per)), jnp.concatenate(x_mid, axis=0))
        x_first = (solved_ref[0].astype(f32) - total).astype(bf16)
        solution_ref[FIRST] = x_first
        solution_ref[MIDDLE] = x_mid_all[row]
        solution_ref[LAST] = x_last_refs[0][...]
        own = solution_ref[...].reshape(levels * width, count)
        result_ref[...] = (sub_ref[...].astype(f32) - dot(up_ref[...], own)).astype(bf16)

    own_solution, result = call(
        solve_backward,
        [shaped(levels, width, count), shaped(*sub.shape)],
        [solved, y_mid, up, sub, *x_lasts, *mid_b, *first],
        scratch=[pltpu.VMEM((rows, width, count), bf16)] * 2,
    )
    return own_solution[None], result[None, None, None]


def solution(mesh):
    return jax.shard_map(
        per_device,
        mesh=mesh,
        in_specs=(
            P("pr", None, None, None),
            P("pr", None, None, None),
            P("pr", None, None, "pc", None, None),
            P(),
            P("gz", "pr", "pc", None, None),
            P("gz", "pr", "pc", None, None),
            P("gz", "pr", "pc", None, None),
        ),
        out_specs=(P("pr", None, None, None), P("gz", "pr", "pc", None, None)),
        check_vma=False,
    )
```

```python
import jax
import jax.numpy as jnp
from jax import lax
from jax.experimental import pallas as pl
from jax.experimental.pallas import tpu as pltpu
from jax.sharding import PartitionSpec as P

FIRST, MIDDLE, LAST = range(3)
VMEM = pl.BlockSpec(memory_space=pltpu.VMEM)
SMEM = pl.BlockSpec(memory_space=pltpu.SMEM)


def dot(a, b):
    return jnp.dot(a, b, preferred_element_type=jnp.float32)


def hop(x, axis, offset):
    size = lax.axis_size(axis)
    return lax.ppermute(x, axis, [(i, i ^ offset) for i in range(size)])


def offsets(axis):
    order, bit = [0], lax.axis_size(axis) // 2
    while bit:
        order += [k ^ bit for k in order]
        bit //= 2
    return order


def gather(x, axis):
    bit = lax.axis_size(axis) // 2
    while bit:
        x = jnp.concatenate([x, hop(x, axis, bit)])
        bit //= 2
    return x


def after(x, *others):
    return lax.optimization_barrier((x, *others))[0]


def spread_direct(x, axis):
    return [x] + [hop(x, axis, k) for k in range(1, lax.axis_size(axis))]


def call(kernel, outs, args, scratch=(), in_specs=None):
    return pl.pallas_call(
        kernel,
        out_shape=outs,
        in_specs=in_specs or [VMEM] * len(args),
        out_specs=[VMEM] * len(outs),
        scratch_shapes=list(scratch),
        compiler_params=pltpu.CompilerParams(vmem_limit_bytes=48 * 1024 * 1024),
    )(*args)


def per_device(sep_rhs, diag_inverse, off_blocks, pattern, sub_solution, couple_low, couple_up):
    rows, cols = lax.axis_size("pr"), lax.axis_size("pc")
    rhs, inverse, blocks = sep_rhs[0], diag_inverse[0], off_blocks[0, :, :, 0]
    sub, low, up = sub_solution[0, 0, 0], couple_low[0, 0, 0], couple_up[0, 0, 0]
    levels, width, count = rhs.shape
    per = blocks.shape[1] // levels
    assert levels == 3 and per * cols == rows
    bf16, f32 = jnp.bfloat16, jnp.float32

    def shaped(*shape):
        return jax.ShapeDtypeStruct(shape, bf16)

    mid_size, row_order, col_order = 2 * per, offsets("pr"), offsets("pc")

    def couple_kernel(low_ref, sub_ref, part_ref):
        part_ref[...] = dot(low_ref[...], sub_ref[...]).astype(bf16).reshape(levels, width, count)

    (part,) = call(couple_kernel, [shaped(levels, width, count)], [low, sub])

    def mask_kernel(pattern_ref, blocks_ref, mid_ref, rest_ref):
        row, col = lax.axis_index("pr"), lax.axis_index("pc")

        def masked(level, b):
            i, j = level * rows + row, b * cols + col
            mark = pattern_ref[i, j] if b // per < level else pattern_ref[j, i]
            return jnp.where(mark == 1, blocks_ref[level, b], jnp.zeros((width, width), bf16))

        for m in range(per):
            mid_ref[m] = masked(MIDDLE, m)
            mid_ref[per + m] = masked(MIDDLE, LAST * per + m)
        for m in range(2 * per):
            rest_ref[m] = masked(LAST, m)
            rest_ref[2 * per + m] = masked(FIRST, per + m)

    mid, rest = call(
        mask_kernel,
        [shaped(2 * per, width, width), shaped(4 * per, width, width)],
        [pattern, blocks],
        in_specs=[SMEM, VMEM],
    )

    bit = 1
    while bit < lax.axis_size("gz"):
        part = part + hop(part, "gz", bit)
        bit *= 2
    parts = [part] + [hop(part, "pc", k) for k in range(cols - 1, 0, -1)]
    mid = jnp.concatenate([mid, hop(mid, "pc", 2)])
    mid = after(mid, part)
    mid = jnp.concatenate([mid, hop(mid, "pc", 1)])
    mid = gather(jnp.concatenate([mid, inverse[MIDDLE][None]]), "pr")
    rest = jnp.concatenate([rest, hop(rest, "pc", 2)])
    rest = after(rest, part)
    rest = jnp.concatenate([rest, hop(rest, "pc", 1)])

    def solve_first(rhs_ref, inverse_ref, *refs):
        out_ref, resid_ref = refs[cols:]
        for level in range(levels):
            total = sum(ref[level].astype(f32) for ref in refs[:cols])
            resid = (rhs_ref[level].astype(f32) - total).astype(bf16)
            if level == FIRST:
                out_ref[0] = dot(inverse_ref[...], resid).astype(bf16)
            elif level == MIDDLE:
                out_ref[1] = resid
            else:
                resid_ref[...] = resid

    solved, resid_last = call(
        solve_first, [shaped(2, width, count), shaped(width, count)], [rhs, inverse[FIRST], *parts]
    )
    gathered = gather(solved, "pr")

    mid_stride = cols * mid_size + 1

    def mid_factor(mid_ref, n, upper):
        picks = [n * mid_stride + c * mid_size + upper * per + m for c in range(cols) for m in range(per)]
        return jnp.concatenate([mid_ref[pick] for pick in picks], axis=1)

    def row_factor(ref, half):
        picks = [c * 4 * per + half * per + m for c in range(cols) for m in range(per)]
        return jnp.concatenate([ref[pick] for pick in picks], axis=1)

    def stack(ref, col):
        return jnp.concatenate([ref[m * cols + (col ^ k)] for k in col_order for m in range(per)], axis=0)

    def solve_forward(inverse_ref, resid_ref, gathered_ref, mid_ref, last_ref, x_last_ref, y_mid_ref, y_first_ref):
        row, col = lax.axis_index("pr"), lax.axis_index("pc")
        for n, k in enumerate(row_order):
            y_first_ref[row ^ k] = gathered_ref[2 * n]
        y_first = stack(y_first_ref, col)
        for n, k in enumerate(row_order):
            resid = (gathered_ref[2 * n + 1].astype(f32) - dot(mid_factor(mid_ref, n, 0), y_first)).astype(bf16)
            y_mid_ref[row ^ k] = dot(mid_ref[n * mid_stride + cols * mid_size], resid).astype(bf16)
        total = dot(row_factor(last_ref, 0), y_first) + dot(row_factor(last_ref, 1), stack(y_mid_ref, col))
        resid = (resid_ref[...].astype(f32) - total).astype(bf16)
        x_last_ref[0] = dot(inverse_ref[...], resid).astype(bf16)

    x_last, y_mid = call(
        solve_forward,
        [shaped(1, width, count), shaped(rows, width, count)],
        [inverse[LAST], resid_last, gathered, mid, rest],
        scratch=[pltpu.VMEM((rows, width, count), bf16)],
    )
    x_lasts = gather(x_last, "pr")

    def solve_backward(solved_ref, y_mid_ref, up_ref, sub_ref, x_lasts_ref, mid_ref, first_ref,
                       solution_ref, result_ref, x_last_all, x_mid_all):
        row, col = lax.axis_index("pr"), lax.axis_index("pc")
        for n, k in enumerate(row_order):
            x_last_all[row ^ k] = x_lasts_ref[n]
        x_last = stack(x_last_all, col)
        for n, k in enumerate(row_order):
            total = dot(mid_factor(mid_ref, n, 1), x_last)
            x_mid_all[row ^ k] = (y_mid_ref[row ^ k].astype(f32) - total).astype(bf16)
        total = dot(row_factor(first_ref, 3), x_last) + dot(row_factor(first_ref, 2), stack(x_mid_all, col))
        solution_ref[FIRST] = (solved_ref[0].astype(f32) - total).astype(bf16)
        solution_ref[MIDDLE] = x_mid_all[row]
        solution_ref[LAST] = x_lasts_ref[0]
        own = solution_ref[...].reshape(levels * width, count)
        result_ref[...] = (sub_ref[...].astype(f32) - dot(up_ref[...], own)).astype(bf16)

    own_solution, result = call(
        solve_backward,
        [shaped(levels, width, count), shaped(*sub.shape)],
        [solved, y_mid, up, sub, x_lasts, mid, rest],
        scratch=[pltpu.VMEM((rows, width, count), bf16)] * 2,
    )
    return own_solution[None], result[None, None, None]


def solution(mesh):
    return jax.shard_map(
        per_device,
        mesh=mesh,
        in_specs=(
            P("pr", None, None, None),
            P("pr", None, None, None),
            P("pr", None, None, "pc", None, None),
            P(),
            P("gz", "pr", "pc", None, None),
            P("gz", "pr", "pc", None, None),
            P("gz", "pr", "pc", None, None),
        ),
        out_specs=(P("pr", None, None, None), P("gz", "pr", "pc", None, None)),
        check_vma=False,
    )
```

```python
import jax
import jax.numpy as jnp
from jax import lax
from jax.experimental import pallas as pl
from jax.experimental.pallas import tpu as pltpu
from jax.sharding import PartitionSpec as P

FIRST, MIDDLE, LAST = range(3)
VMEM = pl.BlockSpec(memory_space=pltpu.VMEM)
SMEM = pl.BlockSpec(memory_space=pltpu.SMEM)


def dot(a, b):
    return jnp.dot(a, b, preferred_element_type=jnp.float32)


def hop(x, axis, offset):
    size = lax.axis_size(axis)
    return lax.ppermute(x, axis, [(i, i ^ offset) for i in range(size)])


def far_to_near(axis):
    bit = lax.axis_size(axis) // 2
    while bit:
        yield bit
        bit //= 2


def offsets(axis):
    order = [0]
    for bit in far_to_near(axis):
        order += [k ^ bit for k in order]
    return order


def far_half(x, axis):
    return jnp.concatenate([x, hop(x, axis, lax.axis_size(axis) // 2)])


def near_half(x, axis):
    for bit in list(far_to_near(axis))[1:]:
        x = jnp.concatenate([x, hop(x, axis, bit)])
    return x


def gather(x, axis):
    return near_half(far_half(x, axis), axis)


def gather_direct(x, axis):
    got = {k: hop(x, axis, k) for k in range(lax.axis_size(axis) - 1, 0, -1)}
    return jnp.concatenate([x] + [got[k] for k in offsets(axis)[1:]])


def after(x, *others):
    return lax.optimization_barrier((x, *others))[0]


def call(kernel, outs, args, scratch=(), in_specs=None):
    return pl.pallas_call(
        kernel,
        out_shape=outs,
        in_specs=in_specs or [VMEM] * len(args),
        out_specs=[VMEM] * len(outs),
        scratch_shapes=list(scratch),
        compiler_params=pltpu.CompilerParams(vmem_limit_bytes=48 * 1024 * 1024),
    )(*args)


def per_device(sep_rhs, diag_inverse, off_blocks, pattern, sub_solution, couple_low, couple_up):
    rows, cols = lax.axis_size("pr"), lax.axis_size("pc")
    rhs, inverse, blocks = sep_rhs[0], diag_inverse[0], off_blocks[0, :, :, 0]
    sub, low, up = sub_solution[0, 0, 0], couple_low[0, 0, 0], couple_up[0, 0, 0]
    levels, width, count = rhs.shape
    per = blocks.shape[1] // levels
    assert levels == 3 and per * cols == rows
    bf16, f32 = jnp.bfloat16, jnp.float32

    def shaped(*shape):
        return jax.ShapeDtypeStruct(shape, bf16)

    row_order, col_order = offsets("pr"), offsets("pc")


    def couple_kernel(low_ref, sub_ref, part_ref, kept_ref):
        kept_ref[...] = sub_ref[...]
        part_ref[...] = dot(low_ref[...], sub_ref[...]).astype(bf16).reshape(levels, width, count)

    part, kept = call(couple_kernel, [shaped(levels, width, count), shaped(*sub.shape)], [low, sub])

    def mask_kernel(pattern_ref, inverse_ref, blocks_ref, early_ref, late_ref, column_ref):
        row, col = lax.axis_index("pr"), lax.axis_index("pc")

        def masked(level, b):
            i, j = level * rows + row, b * cols + col
            mark = pattern_ref[i, j] if b // per < level else pattern_ref[j, i]
            return jnp.where(mark == 1, blocks_ref[level, b], jnp.zeros((width, width), bf16))

        for m in range(per):
            to_first, to_last = masked(MIDDLE, m), masked(MIDDLE, LAST * per + m)
            early_ref[m] = masked(LAST, MIDDLE * per + m)
            early_ref[per + m] = masked(FIRST, MIDDLE * per + m)
            late_ref[m] = masked(LAST, m)
            late_ref[per + m] = masked(FIRST, LAST * per + m)
            late_ref[2 * per + m] = to_last
            late_ref[3 * per + m] = to_first
            column_ref[m] = dot(inverse_ref[...], to_first).astype(bf16)
            column_ref[per + m] = to_last

    early, late, column = call(
        mask_kernel,
        [shaped(2 * per, width, width), shaped(4 * per, width, width), shaped(2 * per, width, width)],
        [pattern, inverse[MIDDLE], after(blocks, part)],
        in_specs=[SMEM, VMEM, VMEM],
    )

    def row_factor(ref, start):
        share = ref.shape[0] // cols
        return jnp.concatenate([ref[c * share + start + m] for c in range(cols) for m in range(per)], axis=1)

    def stack(ref, col):
        return jnp.concatenate([ref[m * cols + (col ^ k)] for k in col_order for m in range(per)], axis=0)

    def fill_kernel(early_ref, late_ref, columns_ref, forward_ref, backward_ref, held_ref):
        row, col = lax.axis_index("pr"), lax.axis_index("pc")
        for start, source, out_ref in ((0, 0, forward_ref), (per, 1, backward_ref)):
            factor = row_factor(early_ref, start)
            for m in range(per):
                for n, k in enumerate(row_order):
                    held_ref[row ^ k] = columns_ref[n * 2 * per + source * per + m]
                fill = dot(factor, stack(held_ref, col))
                out_ref[m] = (late_ref[start + m].astype(f32) - fill).astype(bf16)
        for m in range(per):
            backward_ref[per + m] = late_ref[2 * per + m]
            forward_ref[per + m] = late_ref[3 * per + m]

    def solve_first(rhs_ref, first_inverse_ref, middle_inverse_ref, total_ref, out_ref, resid_ref):
        resid = (rhs_ref[FIRST].astype(f32) - total_ref[FIRST].astype(f32)).astype(bf16)
        out_ref[0] = dot(first_inverse_ref[...], resid).astype(bf16)
        resid = (rhs_ref[MIDDLE].astype(f32) - total_ref[MIDDLE].astype(f32)).astype(bf16)
        out_ref[1] = dot(middle_inverse_ref[...], resid).astype(bf16)
        resid_ref[...] = resid

    early = far_half(early, "pc")
    bit = 1
    while bit < lax.axis_size("gz"):
        part = part + hop(part, "gz", bit)
        bit *= 2
    total = part
    for bit in far_to_near("pc"):
        total = total + hop(total, "pc", bit)
    early = near_half(after(early, part), "pc")
    columns = gather(after(column, part), "pr")
    forward, backward = call(
        fill_kernel,
        [shaped(2 * per, width, width), shaped(2 * per, width, width)],
        [early, late, columns],
        scratch=[pltpu.VMEM((rows, width, width), bf16)],
    )
    solved, resid = call(
        solve_first,
        [shaped(2, width, count), shaped(width, count)],
        [rhs, inverse[FIRST], inverse[MIDDLE], total],
    )
    gathered = gather(solved, "pr")
    forward = gather_direct(forward, "pc")
    backward = far_half(after(backward, solved), "pc")
    backward = near_half(after(backward, gathered), "pc")

    def solve_forward(middle_inverse_ref, last_inverse_ref, rhs_ref, sum_ref, resid_ref, solved_ref, early_ref, late_ref, out_ref,
                      first_ref, middle_ref):
        row, col = lax.axis_index("pr"), lax.axis_index("pc")
        for n, k in enumerate(row_order):
            first_ref[row ^ k] = solved_ref[2 * n]
            middle_ref[row ^ k] = solved_ref[2 * n + 1]
        first = stack(first_ref, col)
        total = dot(row_factor(late_ref, per), first)
        resid = (resid_ref[...].astype(f32) - total).astype(bf16)
        out_ref[1] = dot(middle_inverse_ref[...], resid).astype(bf16)
        total = dot(row_factor(late_ref, 0), first) + dot(row_factor(early_ref, 0), stack(middle_ref, col))
        total += sum_ref[LAST].astype(f32)
        resid = (rhs_ref[...].astype(f32) - total).astype(bf16)
        out_ref[0] = dot(last_inverse_ref[...], resid).astype(bf16)

    (ends,) = call(
        solve_forward,
        [shaped(2, width, count)],
        [inverse[MIDDLE], inverse[LAST], rhs[LAST], total, resid, gathered, early, forward],
        scratch=[pltpu.VMEM((rows, width, count), bf16)] * 2,
    )
    ends = gather(ends, "pr")

    def solve_backward(solved_ref, up_ref, sub_ref, ends_ref, early_ref, late_ref, solution_ref, result_ref, last_ref, middle_ref):
        row, col = lax.axis_index("pr"), lax.axis_index("pc")
        for n, k in enumerate(row_order):
            last_ref[row ^ k] = ends_ref[2 * n]
            middle_ref[row ^ k] = ends_ref[2 * n + 1]
        last = stack(last_ref, col)
        total = dot(row_factor(early_ref, per), stack(middle_ref, col)) + dot(row_factor(late_ref, 0), last)
        solution_ref[FIRST] = (solved_ref[0].astype(f32) - total).astype(bf16)
        total = dot(row_factor(late_ref, per), last)
        solution_ref[MIDDLE] = (ends_ref[1].astype(f32) - total).astype(bf16)
        solution_ref[LAST] = ends_ref[0]
        own = solution_ref[...].reshape(levels * width, count)
        result_ref[...] = (sub_ref[...].astype(f32) - dot(up_ref[...], own)).astype(bf16)

    own_solution, result = call(
        solve_backward,
        [shaped(levels, width, count), shaped(*sub.shape)],
        [solved, up, kept, ends, early, backward],
        scratch=[pltpu.VMEM((rows, width, count), bf16)] * 2,
    )
    return own_solution[None], result[None, None, None]


def solution(mesh):
    return jax.shard_map(
        per_device,
        mesh=mesh,
        in_specs=(
            P("pr", None, None, None),
            P("pr", None, None, None),
            P("pr", None, None, "pc", None, None),
            P(),
            P("gz", "pr", "pc", None, None),
            P("gz", "pr", "pc", None, None),
            P("gz", "pr", "pc", None, None),
        ),
        out_specs=(P("pr", None, None, None), P("gz", "pr", "pc", None, None)),
        check_vma=False,
    )
```

```python
import jax
import jax.numpy as jnp
from jax import lax
from jax.experimental import pallas as pl
from jax.experimental.pallas import tpu as pltpu
from jax.sharding import PartitionSpec as P

FIRST, MIDDLE, LAST = range(3)
VMEM = pl.BlockSpec(memory_space=pltpu.VMEM)
SMEM = pl.BlockSpec(memory_space=pltpu.SMEM)


def dot(a, b):
    return jnp.dot(a, b, preferred_element_type=jnp.float32)


def hop(x, axis, offset):
    size = lax.axis_size(axis)
    return lax.ppermute(x, axis, [(i, i ^ offset) for i in range(size)])


def far_to_near(axis):
    bit = lax.axis_size(axis) // 2
    while bit:
        yield bit
        bit //= 2


def offsets(axis):
    order = [0]
    for bit in far_to_near(axis):
        order += [k ^ bit for k in order]
    return order


def far_half(x, axis):
    return jnp.concatenate([x, hop(x, axis, lax.axis_size(axis) // 2)])


def near_half(x, axis):
    for bit in list(far_to_near(axis))[1:]:
        x = jnp.concatenate([x, hop(x, axis, bit)])
    return x


def gather(x, axis):
    return near_half(far_half(x, axis), axis)


def gather_direct(x, axis):
    got = {k: hop(x, axis, k) for k in range(lax.axis_size(axis) - 1, 0, -1)}
    return jnp.concatenate([x] + [got[k] for k in offsets(axis)[1:]])


def after(x, *others):
    return lax.optimization_barrier((x, *others))[0]


def call(kernel, outs, args, scratch=(), in_specs=None):
    return pl.pallas_call(
        kernel,
        out_shape=outs,
        in_specs=in_specs or [VMEM] * len(args),
        out_specs=[VMEM] * len(outs),
        scratch_shapes=list(scratch),
        compiler_params=pltpu.CompilerParams(vmem_limit_bytes=48 * 1024 * 1024),
    )(*args)


def per_device(sep_rhs, diag_inverse, off_blocks, pattern, sub_solution, couple_low, couple_up):
    rows, cols = lax.axis_size("pr"), lax.axis_size("pc")
    rhs, inverse, blocks = sep_rhs[0], diag_inverse[0], off_blocks[0, :, :, 0]
    sub, low, up = sub_solution[0, 0, 0], couple_low[0, 0, 0], couple_up[0, 0, 0]
    levels, width, count = rhs.shape
    per = blocks.shape[1] // levels
    assert levels == 3 and per * cols == rows
    bf16, f32 = jnp.bfloat16, jnp.float32

    def shaped(*shape):
        return jax.ShapeDtypeStruct(shape, bf16)

    row_order, col_order = offsets("pr"), offsets("pc")


    def couple_kernel(low_ref, sub_ref, part_ref, kept_ref):
        kept_ref[...] = sub_ref[...]
        part_ref[...] = dot(low_ref[...], sub_ref[...]).astype(bf16).reshape(levels, width, count)

    part, kept = call(couple_kernel, [shaped(levels, width, count), shaped(*sub.shape)], [low, sub])

    def mask_kernel(pattern_ref, inverse_ref, blocks_ref, early_ref, late_ref, column_ref):
        row, col = lax.axis_index("pr"), lax.axis_index("pc")

        def masked(level, b):
            i, j = level * rows + row, b * cols + col
            mark = pattern_ref[i, j] if b // per < level else pattern_ref[j, i]
            return jnp.where(mark == 1, blocks_ref[level, b], jnp.zeros((width, width), bf16))

        for m in range(per):
            to_first, to_last = masked(MIDDLE, m), masked(MIDDLE, LAST * per + m)
            early_ref[m] = masked(LAST, MIDDLE * per + m)
            early_ref[per + m] = masked(FIRST, MIDDLE * per + m)
            late_ref[m] = masked(LAST, m)
            late_ref[per + m] = masked(FIRST, LAST * per + m)
            late_ref[2 * per + m] = to_last
            late_ref[3 * per + m] = to_first
            column_ref[m] = dot(inverse_ref[...], to_first).astype(bf16)
            column_ref[per + m] = to_last

    early, late, column = call(
        mask_kernel,
        [shaped(2 * per, width, width), shaped(4 * per, width, width), shaped(2 * per, width, width)],
        [pattern, inverse[MIDDLE], after(blocks, part)],
        in_specs=[SMEM, VMEM, VMEM],
    )

    def row_factor(ref, start):
        share = ref.shape[0] // cols
        return jnp.concatenate([ref[c * share + start + m] for c in range(cols) for m in range(per)], axis=1)

    def stack(ref, col):
        return jnp.concatenate([ref[m * cols + (col ^ k)] for k in col_order for m in range(per)], axis=0)

    def fill_kernel(early_ref, late_ref, columns_ref, forward_ref, backward_ref, held_ref):
        row, col = lax.axis_index("pr"), lax.axis_index("pc")
        for start, source, out_ref in ((0, 0, forward_ref), (per, 1, backward_ref)):
            factor = row_factor(early_ref, start)
            for m in range(per):
                for n, k in enumerate(row_order):
                    held_ref[row ^ k] = columns_ref[n * 2 * per + source * per + m]
                fill = dot(factor, stack(held_ref, col))
                out_ref[m] = (late_ref[start + m].astype(f32) - fill).astype(bf16)
        for m in range(per):
            forward_ref[2 * per + m] = late_ref[2 * per + m]
            forward_ref[per + m] = late_ref[3 * per + m]

    def solve_first(rhs_ref, first_inverse_ref, middle_inverse_ref, total_ref, out_ref, resid_ref):
        resid = (rhs_ref[FIRST].astype(f32) - total_ref[FIRST].astype(f32)).astype(bf16)
        out_ref[0] = dot(first_inverse_ref[...], resid).astype(bf16)
        resid = (rhs_ref[MIDDLE].astype(f32) - total_ref[MIDDLE].astype(f32)).astype(bf16)
        out_ref[1] = dot(middle_inverse_ref[...], resid).astype(bf16)
        resid_ref[...] = resid

    early = far_half(early, "pc")
    bit = 1
    while bit < lax.axis_size("gz"):
        part = part + hop(part, "gz", bit)
        bit *= 2
    total = part
    for bit in far_to_near("pc"):
        total = total + hop(total, "pc", bit)
    early = near_half(after(early, part), "pc")
    columns = gather(after(column, part), "pr")
    forward, backward = call(
        fill_kernel,
        [shaped(3 * per, width, width), shaped(per, width, width)],
        [early, late, columns],
        scratch=[pltpu.VMEM((rows, width, width), bf16)],
    )
    solved, resid = call(
        solve_first,
        [shaped(2, width, count), shaped(width, count)],
        [rhs, inverse[FIRST], inverse[MIDDLE], total],
    )
    gathered = gather(solved, "pr")
    forward = gather_direct(forward, "pc")
    backward = far_half(after(backward, solved), "pc")
    backward = near_half(after(backward, gathered), "pc")

    def solve_forward(middle_inverse_ref, last_inverse_ref, rhs_ref, sum_ref, resid_ref, solved_ref, early_ref, late_ref, out_ref,
                      first_ref, middle_ref):
        row, col = lax.axis_index("pr"), lax.axis_index("pc")
        for n, k in enumerate(row_order):
            first_ref[row ^ k] = solved_ref[2 * n]
            middle_ref[row ^ k] = solved_ref[2 * n + 1]
        first = stack(first_ref, col)
        total = dot(row_factor(late_ref, per), first)
        resid = (resid_ref[...].astype(f32) - total).astype(bf16)
        out_ref[1] = dot(middle_inverse_ref[...], resid).astype(bf16)
        total = dot(row_factor(late_ref, 0), first) + dot(row_factor(early_ref, 0), stack(middle_ref, col))
        total += sum_ref[LAST].astype(f32)
        resid = (rhs_ref[...].astype(f32) - total).astype(bf16)
        out_ref[0] = dot(last_inverse_ref[...], resid).astype(bf16)

    (ends,) = call(
        solve_forward,
        [shaped(2, width, count)],
        [inverse[MIDDLE], inverse[LAST], rhs[LAST], total, resid, gathered, early, forward],
        scratch=[pltpu.VMEM((rows, width, count), bf16)] * 2,
    )
    ends = gather(ends, "pr")

    def solve_backward(solved_ref, up_ref, sub_ref, ends_ref, early_ref, forward_ref, late_ref, solution_ref, result_ref, last_ref, middle_ref):
        row, col = lax.axis_index("pr"), lax.axis_index("pc")
        for n, k in enumerate(row_order):
            last_ref[row ^ k] = ends_ref[2 * n]
            middle_ref[row ^ k] = ends_ref[2 * n + 1]
        last = stack(last_ref, col)
        total = dot(row_factor(early_ref, per), stack(middle_ref, col)) + dot(row_factor(late_ref, 0), last)
        solution_ref[FIRST] = (solved_ref[0].astype(f32) - total).astype(bf16)
        total = dot(row_factor(forward_ref, 2 * per), last)
        solution_ref[MIDDLE] = (ends_ref[1].astype(f32) - total).astype(bf16)
        solution_ref[LAST] = ends_ref[0]
        own = solution_ref[...].reshape(levels * width, count)
        result_ref[...] = (sub_ref[...].astype(f32) - dot(up_ref[...], own)).astype(bf16)

    own_solution, result = call(
        solve_backward,
        [shaped(levels, width, count), shaped(*sub.shape)],
        [solved, up, kept, ends, early, forward, backward],
        scratch=[pltpu.VMEM((rows, width, count), bf16)] * 2,
    )
    return own_solution[None], result[None, None, None]


def solution(mesh):
    return jax.shard_map(
        per_device,
        mesh=mesh,
        in_specs=(
            P("pr", None, None, None),
            P("pr", None, None, None),
            P("pr", None, None, "pc", None, None),
            P(),
            P("gz", "pr", "pc", None, None),
            P("gz", "pr", "pc", None, None),
            P("gz", "pr", "pc", None, None),
        ),
        out_specs=(P("pr", None, None, None), P("gz", "pr", "pc", None, None)),
        check_vma=False,
    )
```

```python
import jax
import jax.numpy as jnp
from jax import lax
from jax.experimental import pallas as pl
from jax.experimental.pallas import tpu as pltpu
from jax.sharding import PartitionSpec as P

FIRST, MIDDLE, LAST = range(3)
VMEM = pl.BlockSpec(memory_space=pltpu.VMEM)
SMEM = pl.BlockSpec(memory_space=pltpu.SMEM)


def dot(a, b):
    return jnp.dot(a, b, preferred_element_type=jnp.float32)


def hop(x, axis, offset):
    size = lax.axis_size(axis)
    return lax.ppermute(x, axis, [(i, i ^ offset) for i in range(size)])


def far_to_near(axis):
    bit = lax.axis_size(axis) // 2
    while bit:
        yield bit
        bit //= 2


def offsets(axis):
    order = [0]
    for bit in far_to_near(axis):
        order += [k ^ bit for k in order]
    return order


def far_half(x, axis):
    return jnp.concatenate([x, hop(x, axis, lax.axis_size(axis) // 2)])


def near_half(x, axis):
    for bit in list(far_to_near(axis))[1:]:
        x = jnp.concatenate([x, hop(x, axis, bit)])
    return x


def gather(x, axis):
    return near_half(far_half(x, axis), axis)


def gather_direct(x, axis):
    got = {k: hop(x, axis, k) for k in range(lax.axis_size(axis) - 1, 0, -1)}
    return jnp.concatenate([x] + [got[k] for k in offsets(axis)[1:]])


def after(x, *others):
    return lax.optimization_barrier((x, *others))[0]


def call(kernel, outs, args, scratch=(), in_specs=None):
    return pl.pallas_call(
        kernel,
        out_shape=outs,
        in_specs=in_specs or [VMEM] * len(args),
        out_specs=[VMEM] * len(outs),
        scratch_shapes=list(scratch),
        compiler_params=pltpu.CompilerParams(vmem_limit_bytes=48 * 1024 * 1024),
    )(*args)


def per_device(sep_rhs, diag_inverse, off_blocks, pattern, sub_solution, couple_low, couple_up):
    rows, cols = lax.axis_size("pr"), lax.axis_size("pc")
    rhs, inverse, blocks = sep_rhs[0], diag_inverse[0], off_blocks[0, :, :, 0]
    sub, low, up = sub_solution[0, 0, 0], couple_low[0, 0, 0], couple_up[0, 0, 0]
    levels, width, count = rhs.shape
    per = blocks.shape[1] // levels
    assert levels == 3 and per * cols == rows
    bf16, f32 = jnp.bfloat16, jnp.float32

    def shaped(*shape):
        return jax.ShapeDtypeStruct(shape, bf16)

    row_order, col_order = offsets("pr"), offsets("pc")


    def couple_kernel(low_ref, sub_ref, part_ref, kept_ref):
        kept_ref[...] = sub_ref[...]
        part_ref[...] = dot(low_ref[...], sub_ref[...]).astype(bf16).reshape(levels, width, count)

    part, kept = call(couple_kernel, [shaped(levels, width, count), shaped(*sub.shape)], [low, sub])

    def masked(pattern_ref, block, level, b):
        i, j = level * rows + lax.axis_index("pr"), b * cols + lax.axis_index("pc")
        if b // per > level:
            i, j = j, i
        spot = [lax.broadcasted_iota(jnp.int32, pattern_ref.shape, axis) == at for axis, at in ((0, i), (1, j))]
        marks = jnp.where(spot[0] & spot[1] & (pattern_ref[...] == 1), 1.0, 0.0)
        return (block.astype(f32) * jnp.max(marks, axis=(0, 1), keepdims=True)).astype(bf16)

    def early_kernel(pattern_ref, blocks_ref, early_ref):
        for m in range(per):
            early_ref[m] = masked(pattern_ref, blocks_ref[LAST, MIDDLE * per + m], LAST, MIDDLE * per + m)
            early_ref[per + m] = masked(pattern_ref, blocks_ref[FIRST, MIDDLE * per + m], FIRST, MIDDLE * per + m)

    def mask_kernel(pattern_ref, inverse_ref, blocks_ref, late_ref, column_ref):
        for m in range(per):
            to_first = masked(pattern_ref, blocks_ref[MIDDLE, m], MIDDLE, m)
            to_last = masked(pattern_ref, blocks_ref[MIDDLE, LAST * per + m], MIDDLE, LAST * per + m)
            late_ref[m] = masked(pattern_ref, blocks_ref[LAST, m], LAST, m)
            late_ref[per + m] = masked(pattern_ref, blocks_ref[FIRST, LAST * per + m], FIRST, LAST * per + m)
            late_ref[2 * per + m] = to_last
            late_ref[3 * per + m] = to_first
            column_ref[m] = dot(inverse_ref[...], to_first).astype(bf16)
            column_ref[per + m] = to_last

    blocks = after(blocks, part)
    (early,) = call(early_kernel, [shaped(2 * per, width, width)], [pattern, blocks])
    late, column = call(
        mask_kernel,
        [shaped(4 * per, width, width), shaped(2 * per, width, width)],
        [pattern, inverse[MIDDLE], blocks],
    )

    def row_factor(ref, start):
        share = ref.shape[0] // cols
        return jnp.concatenate([ref[c * share + start + m] for c in range(cols) for m in range(per)], axis=1)

    def stack(ref, col):
        return jnp.concatenate([ref[m * cols + (col ^ k)] for k in col_order for m in range(per)], axis=0)

    def fill_kernel(early_ref, late_ref, columns_ref, forward_ref, backward_ref, held_ref):
        row, col = lax.axis_index("pr"), lax.axis_index("pc")
        for start, source, out_ref in ((0, 0, forward_ref), (per, 1, backward_ref)):
            factor = row_factor(early_ref, start)
            for m in range(per):
                for n, k in enumerate(row_order):
                    held_ref[row ^ k] = columns_ref[n * 2 * per + source * per + m]
                fill = dot(factor, stack(held_ref, col))
                out_ref[m] = (late_ref[start + m].astype(f32) - fill).astype(bf16)
        for m in range(per):
            forward_ref[2 * per + m] = late_ref[2 * per + m]
            forward_ref[per + m] = late_ref[3 * per + m]

    def solve_first(rhs_ref, first_inverse_ref, middle_inverse_ref, total_ref, out_ref, resid_ref):
        resid = (rhs_ref[FIRST].astype(f32) - total_ref[FIRST].astype(f32)).astype(bf16)
        out_ref[0] = dot(first_inverse_ref[...], resid).astype(bf16)
        resid = (rhs_ref[MIDDLE].astype(f32) - total_ref[MIDDLE].astype(f32)).astype(bf16)
        out_ref[1] = dot(middle_inverse_ref[...], resid).astype(bf16)
        resid_ref[...] = resid

    early = far_half(early, "pc")
    bit = 1
    while bit < lax.axis_size("gz"):
        part = part + hop(part, "gz", bit)
        bit *= 2
    total = part
    for bit in far_to_near("pc"):
        total = total + hop(total, "pc", bit)
    early = near_half(after(early, part), "pc")
    columns = gather(after(column, part), "pr")
    forward, backward = call(
        fill_kernel,
        [shaped(3 * per, width, width), shaped(per, width, width)],
        [early, late, columns],
        scratch=[pltpu.VMEM((rows, width, width), bf16)],
    )
    solved, resid = call(
        solve_first,
        [shaped(2, width, count), shaped(width, count)],
        [rhs, inverse[FIRST], inverse[MIDDLE], total],
    )
    gathered = gather(solved, "pr")
    forward = gather_direct(forward, "pc")
    backward = far_half(after(backward, solved), "pc")
    backward = near_half(after(backward, gathered), "pc")

    def solve_forward(middle_inverse_ref, last_inverse_ref, rhs_ref, sum_ref, resid_ref, solved_ref, early_ref, late_ref, out_ref,
                      first_ref, middle_ref):
        row, col = lax.axis_index("pr"), lax.axis_index("pc")
        for n, k in enumerate(row_order):
            first_ref[row ^ k] = solved_ref[2 * n]
            middle_ref[row ^ k] = solved_ref[2 * n + 1]
        first = stack(first_ref, col)
        total = dot(row_factor(late_ref, per), first)
        resid = (resid_ref[...].astype(f32) - total).astype(bf16)
        out_ref[1] = dot(middle_inverse_ref[...], resid).astype(bf16)
        total = dot(row_factor(late_ref, 0), first) + dot(row_factor(early_ref, 0), stack(middle_ref, col))
        total += sum_ref[LAST].astype(f32)
        resid = (rhs_ref[...].astype(f32) - total).astype(bf16)
        out_ref[0] = dot(last_inverse_ref[...], resid).astype(bf16)

    (ends,) = call(
        solve_forward,
        [shaped(2, width, count)],
        [inverse[MIDDLE], inverse[LAST], rhs[LAST], total, resid, gathered, early, forward],
        scratch=[pltpu.VMEM((rows, width, count), bf16)] * 2,
    )
    ends = gather(ends, "pr")

    def solve_backward(solved_ref, up_ref, sub_ref, ends_ref, early_ref, forward_ref, late_ref, solution_ref, result_ref, last_ref, middle_ref):
        row, col = lax.axis_index("pr"), lax.axis_index("pc")
        for n, k in enumerate(row_order):
            last_ref[row ^ k] = ends_ref[2 * n]
            middle_ref[row ^ k] = ends_ref[2 * n + 1]
        last = stack(last_ref, col)
        total = dot(row_factor(early_ref, per), stack(middle_ref, col)) + dot(row_factor(late_ref, 0), last)
        solution_ref[FIRST] = (solved_ref[0].astype(f32) - total).astype(bf16)
        total = dot(row_factor(forward_ref, 2 * per), last)
        solution_ref[MIDDLE] = (ends_ref[1].astype(f32) - total).astype(bf16)
        solution_ref[LAST] = ends_ref[0]
        own = solution_ref[...].reshape(levels * width, count)
        result_ref[...] = (sub_ref[...].astype(f32) - dot(up_ref[...], own)).astype(bf16)

    own_solution, result = call(
        solve_backward,
        [shaped(levels, width, count), shaped(*sub.shape)],
        [solved, up, kept, ends, early, forward, backward],
        scratch=[pltpu.VMEM((rows, width, count), bf16)] * 2,
    )
    return own_solution[None], result[None, None, None]


def solution(mesh):
    return jax.shard_map(
        per_device,
        mesh=mesh,
        in_specs=(
            P("pr", None, None, None),
            P("pr", None, None, None),
            P("pr", None, None, "pc", None, None),
            P(),
            P("gz", "pr", "pc", None, None),
            P("gz", "pr", "pc", None, None),
            P("gz", "pr", "pc", None, None),
        ),
        out_specs=(P("pr", None, None, None), P("gz", "pr", "pc", None, None)),
        check_vma=False,
    )
```

```python
import jax
import jax.numpy as jnp
from jax import lax
from jax.experimental import pallas as pl
from jax.experimental.pallas import tpu as pltpu
from jax.sharding import PartitionSpec as P

FIRST, MIDDLE, LAST = range(3)
VMEM = pl.BlockSpec(memory_space=pltpu.VMEM)
SMEM = pl.BlockSpec(memory_space=pltpu.SMEM)


def dot(a, b):
    return jnp.dot(a, b, preferred_element_type=jnp.float32)


def hop(x, axis, offset):
    size = lax.axis_size(axis)
    return lax.ppermute(x, axis, [(i, i ^ offset) for i in range(size)])


def far_to_near(axis):
    bit = lax.axis_size(axis) // 2
    while bit:
        yield bit
        bit //= 2


def offsets(axis):
    order = [0]
    for bit in far_to_near(axis):
        order += [k ^ bit for k in order]
    return order


def far_half(x, axis):
    return jnp.concatenate([x, hop(x, axis, lax.axis_size(axis) // 2)])


def near_half(x, axis):
    for bit in list(far_to_near(axis))[1:]:
        x = jnp.concatenate([x, hop(x, axis, bit)])
    return x


def gather(x, axis):
    return near_half(far_half(x, axis), axis)


def gather_direct(x, axis):
    got = {k: hop(x, axis, k) for k in range(lax.axis_size(axis) - 1, 0, -1)}
    return jnp.concatenate([x] + [got[k] for k in offsets(axis)[1:]])


def after(x, *others):
    return lax.optimization_barrier((x, *others))[0]


def call(kernel, outs, args, scratch=(), in_specs=None):
    return pl.pallas_call(
        kernel,
        out_shape=outs,
        in_specs=in_specs or [VMEM] * len(args),
        out_specs=[VMEM] * len(outs),
        scratch_shapes=list(scratch),
        compiler_params=pltpu.CompilerParams(vmem_limit_bytes=48 * 1024 * 1024),
    )(*args)


def per_device(sep_rhs, diag_inverse, off_blocks, pattern, sub_solution, couple_low, couple_up):
    rows, cols = lax.axis_size("pr"), lax.axis_size("pc")
    rhs, inverse, blocks = sep_rhs[0], diag_inverse[0], off_blocks[0, :, :, 0]
    sub, low, up = sub_solution[0, 0, 0], couple_low[0, 0, 0], couple_up[0, 0, 0]
    levels, width, count = rhs.shape
    per = blocks.shape[1] // levels
    assert levels == 3 and per * cols == rows
    bf16, f32 = jnp.bfloat16, jnp.float32

    def shaped(*shape):
        return jax.ShapeDtypeStruct(shape, bf16)

    row_order, col_order = offsets("pr"), offsets("pc")


    part = dot(low, sub).astype(bf16).reshape(levels, width, count)

    def masked(pattern_ref, block, level, b):
        i, j = level * rows + lax.axis_index("pr"), b * cols + lax.axis_index("pc")
        if b // per > level:
            i, j = j, i
        spot = [lax.broadcasted_iota(jnp.int32, pattern_ref.shape, axis) == at for axis, at in ((0, i), (1, j))]
        marks = jnp.where(spot[0] & spot[1] & (pattern_ref[...] == 1), 1.0, 0.0)
        return (block.astype(f32) * jnp.max(marks, axis=(0, 1), keepdims=True)).astype(bf16)

    def early_kernel(pattern_ref, blocks_ref, early_ref):
        for m in range(per):
            early_ref[m] = masked(pattern_ref, blocks_ref[LAST, MIDDLE * per + m], LAST, MIDDLE * per + m)
            early_ref[per + m] = masked(pattern_ref, blocks_ref[FIRST, MIDDLE * per + m], FIRST, MIDDLE * per + m)

    def mask_kernel(pattern_ref, inverse_ref, blocks_ref, sub_ref, late_ref, column_ref, kept_ref):
        kept_ref[...] = sub_ref[...]
        for m in range(per):
            to_first = masked(pattern_ref, blocks_ref[MIDDLE, m], MIDDLE, m)
            to_last = masked(pattern_ref, blocks_ref[MIDDLE, LAST * per + m], MIDDLE, LAST * per + m)
            late_ref[m] = masked(pattern_ref, blocks_ref[LAST, m], LAST, m)
            late_ref[per + m] = masked(pattern_ref, blocks_ref[FIRST, LAST * per + m], FIRST, LAST * per + m)
            late_ref[2 * per + m] = to_last
            late_ref[3 * per + m] = to_first
            column_ref[m] = dot(inverse_ref[...], to_first).astype(bf16)
            column_ref[per + m] = to_last

    blocks = after(blocks, part)
    (early,) = call(early_kernel, [shaped(2 * per, width, width)], [pattern, blocks])
    late, column, kept = call(
        mask_kernel,
        [shaped(4 * per, width, width), shaped(2 * per, width, width), shaped(*sub.shape)],
        [pattern, inverse[MIDDLE], blocks, sub],
    )

    def row_factor(ref, start):
        share = ref.shape[0] // cols
        return jnp.concatenate([ref[c * share + start + m] for c in range(cols) for m in range(per)], axis=1)

    def stack(ref, col):
        return jnp.concatenate([ref[m * cols + (col ^ k)] for k in col_order for m in range(per)], axis=0)

    def fill_kernel(early_ref, late_ref, columns_ref, forward_ref, backward_ref, held_ref):
        row, col = lax.axis_index("pr"), lax.axis_index("pc")
        for start, source, out_ref in ((0, 0, forward_ref), (per, 1, backward_ref)):
            factor = row_factor(early_ref, start)
            for m in range(per):
                for n, k in enumerate(row_order):
                    held_ref[row ^ k] = columns_ref[n * 2 * per + source * per + m]
                fill = dot(factor, stack(held_ref, col))
                out_ref[m] = (late_ref[start + m].astype(f32) - fill).astype(bf16)
        for m in range(per):
            forward_ref[2 * per + m] = late_ref[2 * per + m]
            forward_ref[per + m] = late_ref[3 * per + m]

    def solve_first(rhs_ref, first_inverse_ref, middle_inverse_ref, total_ref, out_ref, resid_ref):
        resid = (rhs_ref[FIRST].astype(f32) - total_ref[FIRST].astype(f32)).astype(bf16)
        out_ref[0] = dot(first_inverse_ref[...], resid).astype(bf16)
        resid = (rhs_ref[MIDDLE].astype(f32) - total_ref[MIDDLE].astype(f32)).astype(bf16)
        out_ref[1] = dot(middle_inverse_ref[...], resid).astype(bf16)
        resid_ref[...] = resid

    early = far_half(early, "pc")
    bit = 1
    while bit < lax.axis_size("gz"):
        part = part + hop(part, "gz", bit)
        bit *= 2
    total = part
    for bit in far_to_near("pc"):
        total = total + hop(total, "pc", bit)
    early = near_half(after(early, part), "pc")
    columns = gather(after(column, part), "pr")
    forward, backward = call(
        fill_kernel,
        [shaped(3 * per, width, width), shaped(per, width, width)],
        [early, late, columns],
        scratch=[pltpu.VMEM((rows, width, width), bf16)],
    )
    solved, resid = call(
        solve_first,
        [shaped(2, width, count), shaped(width, count)],
        [rhs, inverse[FIRST], inverse[MIDDLE], total],
    )
    gathered = gather(solved, "pr")
    forward = gather_direct(forward, "pc")
    backward = far_half(after(backward, solved), "pc")
    backward = near_half(after(backward, gathered), "pc")

    def solve_forward(middle_inverse_ref, last_inverse_ref, rhs_ref, sum_ref, resid_ref, solved_ref, early_ref, late_ref, out_ref,
                      first_ref, middle_ref):
        row, col = lax.axis_index("pr"), lax.axis_index("pc")
        for n, k in enumerate(row_order):
            first_ref[row ^ k] = solved_ref[2 * n]
            middle_ref[row ^ k] = solved_ref[2 * n + 1]
        first = stack(first_ref, col)
        total = dot(row_factor(late_ref, per), first)
        resid = (resid_ref[...].astype(f32) - total).astype(bf16)
        out_ref[1] = dot(middle_inverse_ref[...], resid).astype(bf16)
        total = dot(row_factor(late_ref, 0), first) + dot(row_factor(early_ref, 0), stack(middle_ref, col))
        total += sum_ref[LAST].astype(f32)
        resid = (rhs_ref[...].astype(f32) - total).astype(bf16)
        out_ref[0] = dot(last_inverse_ref[...], resid).astype(bf16)

    (ends,) = call(
        solve_forward,
        [shaped(2, width, count)],
        [inverse[MIDDLE], inverse[LAST], rhs[LAST], total, resid, gathered, early, forward],
        scratch=[pltpu.VMEM((rows, width, count), bf16)] * 2,
    )
    ends = gather(ends, "pr")

    def solve_backward(solved_ref, up_ref, sub_ref, ends_ref, early_ref, forward_ref, late_ref, solution_ref, result_ref, last_ref, middle_ref):
        row, col = lax.axis_index("pr"), lax.axis_index("pc")
        for n, k in enumerate(row_order):
            last_ref[row ^ k] = ends_ref[2 * n]
            middle_ref[row ^ k] = ends_ref[2 * n + 1]
        last = stack(last_ref, col)
        total = dot(row_factor(early_ref, per), stack(middle_ref, col)) + dot(row_factor(late_ref, 0), last)
        solution_ref[FIRST] = (solved_ref[0].astype(f32) - total).astype(bf16)
        total = dot(row_factor(forward_ref, 2 * per), last)
        solution_ref[MIDDLE] = (ends_ref[1].astype(f32) - total).astype(bf16)
        solution_ref[LAST] = ends_ref[0]
        own = solution_ref[...].reshape(levels * width, count)
        result_ref[...] = (sub_ref[...].astype(f32) - dot(up_ref[...], own)).astype(bf16)

    own_solution, result = call(
        solve_backward,
        [shaped(levels, width, count), shaped(*sub.shape)],
        [solved, up, kept, ends, early, forward, backward],
        scratch=[pltpu.VMEM((rows, width, count), bf16)] * 2,
    )
    return own_solution[None], result[None, None, None]


def solution(mesh):
    return jax.shard_map(
        per_device,
        mesh=mesh,
        in_specs=(
            P("pr", None, None, None),
            P("pr", None, None, None),
            P("pr", None, None, "pc", None, None),
            P(),
            P("gz", "pr", "pc", None, None),
            P("gz", "pr", "pc", None, None),
            P("gz", "pr", "pc", None, None),
        ),
        out_specs=(P("pr", None, None, None), P("gz", "pr", "pc", None, None)),
        check_vma=False,
    )
```

```python
import jax
import jax.numpy as jnp
from jax import lax
from jax.experimental import pallas as pl
from jax.experimental.pallas import tpu as pltpu
from jax.sharding import PartitionSpec as P

FIRST, MIDDLE, LAST = range(3)
VMEM = pl.BlockSpec(memory_space=pltpu.VMEM)
SMEM = pl.BlockSpec(memory_space=pltpu.SMEM)


def dot(a, b):
    return jnp.dot(a, b, preferred_element_type=jnp.float32)


def hop(x, axis, offset):
    size = lax.axis_size(axis)
    return lax.ppermute(x, axis, [(i, i ^ offset) for i in range(size)])


def far_to_near(axis):
    bit = lax.axis_size(axis) // 2
    while bit:
        yield bit
        bit //= 2


def offsets(axis):
    order = [0]
    for bit in far_to_near(axis):
        order += [k ^ bit for k in order]
    return order


def far_half(x, axis):
    return jnp.concatenate([x, hop(x, axis, lax.axis_size(axis) // 2)])


def near_half(x, axis):
    for bit in list(far_to_near(axis))[1:]:
        x = jnp.concatenate([x, hop(x, axis, bit)])
    return x


def gather(x, axis):
    return near_half(far_half(x, axis), axis)


def gather_direct(x, axis):
    got = {k: hop(x, axis, k) for k in range(lax.axis_size(axis) - 1, 0, -1)}
    return jnp.concatenate([x] + [got[k] for k in offsets(axis)[1:]])


def after(x, *others):
    return lax.optimization_barrier((x, *others))[0]


def call(kernel, outs, args, scratch=(), in_specs=None):
    return pl.pallas_call(
        kernel,
        out_shape=outs,
        in_specs=in_specs or [VMEM] * len(args),
        out_specs=[VMEM] * len(outs),
        scratch_shapes=list(scratch),
        compiler_params=pltpu.CompilerParams(vmem_limit_bytes=48 * 1024 * 1024),
    )(*args)


def per_device(sep_rhs, diag_inverse, off_blocks, pattern, sub_solution, couple_low, couple_up):
    rows, cols = lax.axis_size("pr"), lax.axis_size("pc")
    rhs, inverse, blocks = sep_rhs[0], diag_inverse[0], off_blocks[0, :, :, 0]
    sub, low, up = sub_solution[0, 0, 0], couple_low[0, 0, 0], couple_up[0, 0, 0]
    levels, width, count = rhs.shape
    per = blocks.shape[1] // levels
    assert levels == 3 and per * cols == rows
    bf16, f32 = jnp.bfloat16, jnp.float32

    def shaped(*shape):
        return jax.ShapeDtypeStruct(shape, bf16)

    row_order, col_order = offsets("pr"), offsets("pc")


    part = dot(after(low, sub), sub).astype(bf16).reshape(levels, width, count)

    def masked(pattern_ref, block, level, b):
        i, j = level * rows + lax.axis_index("pr"), b * cols + lax.axis_index("pc")
        if b // per > level:
            i, j = j, i
        spot = [lax.broadcasted_iota(jnp.int32, pattern_ref.shape, axis) == at for axis, at in ((0, i), (1, j))]
        marks = jnp.where(spot[0] & spot[1] & (pattern_ref[...] == 1), 1.0, 0.0)
        return (block.astype(f32) * jnp.max(marks, axis=(0, 1), keepdims=True)).astype(bf16)

    def early_kernel(pattern_ref, blocks_ref, early_ref):
        for m in range(per):
            early_ref[m] = masked(pattern_ref, blocks_ref[LAST, MIDDLE * per + m], LAST, MIDDLE * per + m)
            early_ref[per + m] = masked(pattern_ref, blocks_ref[FIRST, MIDDLE * per + m], FIRST, MIDDLE * per + m)

    def mask_kernel(pattern_ref, inverse_ref, blocks_ref, sub_ref, late_ref, column_ref, kept_ref):
        kept_ref[...] = sub_ref[...]
        for m in range(per):
            to_first = masked(pattern_ref, blocks_ref[MIDDLE, m], MIDDLE, m)
            to_last = masked(pattern_ref, blocks_ref[MIDDLE, LAST * per + m], MIDDLE, LAST * per + m)
            late_ref[m] = masked(pattern_ref, blocks_ref[LAST, m], LAST, m)
            late_ref[per + m] = masked(pattern_ref, blocks_ref[FIRST, LAST * per + m], FIRST, LAST * per + m)
            late_ref[2 * per + m] = to_last
            late_ref[3 * per + m] = to_first
            column_ref[m] = dot(inverse_ref[...], to_first).astype(bf16)
            column_ref[per + m] = to_last

    blocks = after(blocks, part)
    (early,) = call(early_kernel, [shaped(2 * per, width, width)], [pattern, blocks])
    late, column, kept = call(
        mask_kernel,
        [shaped(4 * per, width, width), shaped(2 * per, width, width), shaped(*sub.shape)],
        [pattern, inverse[MIDDLE], blocks, sub],
    )

    def row_factor(ref, start):
        share = ref.shape[0] // cols
        return jnp.concatenate([ref[c * share + start + m] for c in range(cols) for m in range(per)], axis=1)

    def stack(ref, col):
        return jnp.concatenate([ref[m * cols + (col ^ k)] for k in col_order for m in range(per)], axis=0)

    def fill_kernel(early_ref, late_ref, columns_ref, forward_ref, backward_ref, held_ref):
        row, col = lax.axis_index("pr"), lax.axis_index("pc")
        for start, source, out_ref in ((0, 0, forward_ref), (per, 1, backward_ref)):
            factor = row_factor(early_ref, start)
            for m in range(per):
                for n, k in enumerate(row_order):
                    held_ref[row ^ k] = columns_ref[n * 2 * per + source * per + m]
                fill = dot(factor, stack(held_ref, col))
                out_ref[m] = (late_ref[start + m].astype(f32) - fill).astype(bf16)
        for m in range(per):
            forward_ref[2 * per + m] = late_ref[2 * per + m]
            forward_ref[per + m] = late_ref[3 * per + m]

    def solve_first(rhs_ref, first_inverse_ref, middle_inverse_ref, total_ref, out_ref, resid_ref):
        resid = (rhs_ref[FIRST].astype(f32) - total_ref[FIRST].astype(f32)).astype(bf16)
        out_ref[0] = dot(first_inverse_ref[...], resid).astype(bf16)
        resid = (rhs_ref[MIDDLE].astype(f32) - total_ref[MIDDLE].astype(f32)).astype(bf16)
        out_ref[1] = dot(middle_inverse_ref[...], resid).astype(bf16)
        resid_ref[...] = resid

    early = far_half(early, "pc")
    bit = 1
    while bit < lax.axis_size("gz"):
        part = part + hop(part, "gz", bit)
        bit *= 2
    total = part
    for bit in far_to_near("pc"):
        total = total + hop(total, "pc", bit)
    early = near_half(after(early, part), "pc")
    columns = gather(after(column, part), "pr")
    forward, backward = call(
        fill_kernel,
        [shaped(3 * per, width, width), shaped(per, width, width)],
        [early, late, columns],
        scratch=[pltpu.VMEM((rows, width, width), bf16)],
    )
    solved, resid = call(
        solve_first,
        [shaped(2, width, count), shaped(width, count)],
        [rhs, inverse[FIRST], inverse[MIDDLE], total],
    )
    gathered = gather(solved, "pr")
    forward = gather_direct(forward, "pc")
    backward = far_half(after(backward, solved), "pc")
    backward = near_half(after(backward, gathered), "pc")

    def solve_forward(middle_inverse_ref, last_inverse_ref, rhs_ref, sum_ref, resid_ref, solved_ref, early_ref, late_ref, out_ref,
                      first_ref, middle_ref):
        row, col = lax.axis_index("pr"), lax.axis_index("pc")
        for n, k in enumerate(row_order):
            first_ref[row ^ k] = solved_ref[2 * n]
            middle_ref[row ^ k] = solved_ref[2 * n + 1]
        first = stack(first_ref, col)
        total = dot(row_factor(late_ref, per), first)
        resid = (resid_ref[...].astype(f32) - total).astype(bf16)
        out_ref[1] = dot(middle_inverse_ref[...], resid).astype(bf16)
        total = dot(row_factor(late_ref, 0), first) + dot(row_factor(early_ref, 0), stack(middle_ref, col))
        total += sum_ref[LAST].astype(f32)
        resid = (rhs_ref[...].astype(f32) - total).astype(bf16)
        out_ref[0] = dot(last_inverse_ref[...], resid).astype(bf16)

    (ends,) = call(
        solve_forward,
        [shaped(2, width, count)],
        [inverse[MIDDLE], inverse[LAST], rhs[LAST], total, resid, gathered, early, forward],
        scratch=[pltpu.VMEM((rows, width, count), bf16)] * 2,
    )
    ends = gather(ends, "pr")

    def solve_backward(solved_ref, up_ref, sub_ref, ends_ref, early_ref, forward_ref, late_ref, solution_ref, result_ref, last_ref, middle_ref):
        row, col = lax.axis_index("pr"), lax.axis_index("pc")
        for n, k in enumerate(row_order):
            last_ref[row ^ k] = ends_ref[2 * n]
            middle_ref[row ^ k] = ends_ref[2 * n + 1]
        last = stack(last_ref, col)
        total = dot(row_factor(early_ref, per), stack(middle_ref, col)) + dot(row_factor(late_ref, 0), last)
        solution_ref[FIRST] = (solved_ref[0].astype(f32) - total).astype(bf16)
        total = dot(row_factor(forward_ref, 2 * per), last)
        solution_ref[MIDDLE] = (ends_ref[1].astype(f32) - total).astype(bf16)
        solution_ref[LAST] = ends_ref[0]
        own = solution_ref[...].reshape(levels * width, count)
        result_ref[...] = (sub_ref[...].astype(f32) - dot(up_ref[...], own)).astype(bf16)

    own_solution, result = call(
        solve_backward,
        [shaped(levels, width, count), shaped(*sub.shape)],
        [solved, up, kept, ends, early, forward, backward],
        scratch=[pltpu.VMEM((rows, width, count), bf16)] * 2,
    )
    return own_solution[None], result[None, None, None]


def solution(mesh):
    return jax.shard_map(
        per_device,
        mesh=mesh,
        in_specs=(
            P("pr", None, None, None),
            P("pr", None, None, None),
            P("pr", None, None, "pc", None, None),
            P(),
            P("gz", "pr", "pc", None, None),
            P("gz", "pr", "pc", None, None),
            P("gz", "pr", "pc", None, None),
        ),
        out_specs=(P("pr", None, None, None), P("gz", "pr", "pc", None, None)),
        check_vma=False,
    )
```
